32 devices in a mesh: grp: 2 (over y), dp: 4 (over z), test: 2 (over x), seq: 2 (over core).
Axes of the slice: x: 2, y: 2, z: 4, core: 2. Of those that a mesh axis runs over, the one named last changes fastest.
Arguments:
- train_inputs: bfloat16 [16, 256, 4096], P(('grp', 'dp', 'test'), 'seq'), parts along dimension 0, may hold values from -48 to 48
- train_grads: bfloat16 [16, 256, 7168], P(('grp', 'dp', 'test'), 'seq'), parts along dimension 0, may hold values from -48 to 48
- lengths: int32 [16], P(('grp', 'dp', 'test')), parts along dimension 0, may hold values from 64 to 256, as said below
- proj_in: bfloat16 [64, 4096], replicated, may hold values from -4 to 4
- proj_out: bfloat16 [64, 7168], replicated, may hold values from -4 to 4
- test_grads: float32 [32, 4096], P(('grp', 'dp', 'test')), parts along dimension 0, may hold values from -0.03 to 0.03
Outputs:
- scores: float32 [32, 8], P(('grp', 'dp', 'test')), parts along dimension 0
The draws below stay inside these ranges and needn't reach their ends.
There are 2 independent parts, one for each index of `grp`. The reference program is written for one: setup_inputs(seed, part) draws one part's arguments, and reference() takes and returns one part's arrays. A program takes and returns all parts, laid end to end along the dimension named above; an argument that names none is the same for every part. Nothing has to cross between parts.
Inputs may be any that keep to these rules, and one draw needn't show every extreme that they name: Sequence s holds real tokens in its first lengths[s] slots; some sequence is full.
All inputs are finite; a program needn't handle non-finite values.
Results may differ from the reference program's by a relative error of at most 0.0003.
Values sent between devices are 32-bit elements; how exact they have to be, the bound alone decides.
A program may use at most 64 MiB of HBM per device.

```python
import math
import jax
import jax.numpy as jnp
from jax import lax

D = 4096
FF = 7168
KI = 64
KO = 64
LEN = 256
SEQS = 8
TESTS = 16


def token_scales(key, rise):
    factor = jnp.exp(jax.random.uniform(key, (SEQS, LEN, 1), jnp.float32, math.log(0.5), math.log(2.0)))
    ramp = 1.0 + rise * jnp.arange(SEQS, dtype=jnp.float32) / max(SEQS - 1, 1)
    return factor * ramp[:, None, None]


def draw_tokens(key, width):
    key_base, key_scale = jax.random.split(key)
    base = jax.random.normal(key_base, (SEQS, LEN, width), jnp.float32)
    rise = 2.0
    return (base * token_scales(key_scale, rise)).astype(jnp.bfloat16)


def draw_train_inputs(key, part):
    key = jax.random.fold_in(key, 11)
    return draw_tokens(key, D)


def draw_train_grads(key, part):
    key = jax.random.fold_in(key, 12)
    return draw_tokens(key, FF)


def draw_lengths(key, part):
    key = jax.random.fold_in(key, 13)
    key_vals, key_pick = jax.random.split(key)
    values = jax.random.randint(key_vals, (SEQS,), LEN // 4, LEN + 1)
    chosen = jax.random.randint(key_pick, (), 0, SEQS)
    return jnp.where(jnp.arange(SEQS) == chosen, LEN, values).astype(jnp.int32)


def draw_projection(key, rows, width):
    key_rows, key_common, key_own = jax.random.split(key, 3)
    row_scale = jnp.exp(jax.random.uniform(key_rows, (rows, 1), jnp.float32, math.log(0.3), math.log(3.0)))
    common = jax.random.normal(key_common, (1, width), jnp.float32)
    own = jax.random.normal(key_own, (rows, width), jnp.float32)
    return (row_scale * (own + 0.6 * common) / math.sqrt(width)).astype(jnp.bfloat16)


def draw_proj_in(key, part):
    key = jax.random.fold_in(key, 17)
    return draw_projection(key, KI, D)


def draw_proj_out(key, part):
    key = jax.random.fold_in(key, 19)
    return draw_projection(key, KO, FF)


def levels(stream_key, extent, pieces, low, top_value):
    def one(axis_at, parts):
        heights = jax.random.uniform(jax.random.fold_in(jax.random.fold_in(stream_key, 6), axis_at), (parts,), jnp.float32, low / len(pieces), top_value / len(pieces))
        return jnp.repeat(jnp.exp(heights), extent[axis_at] // parts).reshape((-1,) + (1,) * (len(extent) - axis_at - 1))

    loudness = one(*pieces[0])
    for cut in pieces[1:]:
        loudness = loudness * one(*cut)
    return loudness


def bell_draw(rng, extent, spread, most, cuts=(), held_as=jnp.bfloat16):
    values = spread * jax.random.normal(rng, extent, jnp.float32)
    if cuts:
        values = values * levels(rng, extent, cuts, -0.22, 0.18)
    return jnp.clip(values, -most, most).astype(held_as)


def setup_inputs(seed: int = 0, part: int = 0) -> dict:
    key_list = jax.random.split(jax.random.key(seed), 7)
    part_splits = jax.random.split(jax.random.fold_in(key_list[6], part), 7)
    train_inputs = draw_train_inputs(jax.random.fold_in(jax.random.fold_in(key_list[6], part), 71), part)
    train_grads = draw_train_grads(jax.random.fold_in(jax.random.fold_in(key_list[6], part), 71), part)
    lengths = draw_lengths(jax.random.fold_in(jax.random.fold_in(key_list[6], part), 71), part)
    proj_in = draw_proj_in(jax.random.fold_in(key_list[6], 71), part)
    proj_out = draw_proj_out(jax.random.fold_in(key_list[6], 71), part)
    test_grads = bell_draw(part_splits[5], (TESTS, KO * KI), 0.005, 0.03, ((0, 8),), jnp.float32)
    return dict(train_inputs=train_inputs, train_grads=train_grads, lengths=lengths, proj_in=proj_in, proj_out=proj_out, test_grads=test_grads)


damping = 0.1

def damped_inverse(covariance, token_count):
    width = covariance.shape[0]
    normed = covariance / token_count
    shift = damping * jnp.trace(normed) / width
    damped = normed + shift * jnp.eye(width, dtype=jnp.float32)
    factor = jnp.linalg.cholesky(damped)
    return jax.scipy.linalg.cho_solve((factor, True), jnp.eye(width, dtype=jnp.float32))

def reference(train_inputs, train_grads, lengths, proj_in, proj_out, test_grads):
    positions = jnp.arange(LEN, dtype=jnp.int32)
    valid = (positions[None, :] < lengths[:, None]).astype(jnp.float32)
    highest = lax.Precision.HIGHEST

    def project_sequence(item):
        inputs_seq, grads_seq, valid_seq = item
        inputs_low = jnp.dot(proj_in.astype(jnp.float32), inputs_seq.T.astype(jnp.float32), preferred_element_type=jnp.float32) * valid_seq[None, :]
        grads_low = jnp.dot(proj_out.astype(jnp.float32), grads_seq.T.astype(jnp.float32), preferred_element_type=jnp.float32) * valid_seq[None, :]
        example = jnp.dot(grads_low, inputs_low.T, precision=highest)
        cov_in = jnp.dot(inputs_low, inputs_low.T, precision=highest)
        cov_out = jnp.dot(grads_low, grads_low.T, precision=highest)
        return (example, cov_in, cov_out)
    example_grad, cov_in_all, cov_out_all = lax.map(project_sequence, (train_inputs, train_grads, valid))
    token_count = jnp.sum(valid)
    inv_in = damped_inverse(jnp.sum(cov_in_all, axis=0), token_count)
    inv_out = damped_inverse(jnp.sum(cov_out_all, axis=0), token_count)
    shaped = jnp.matmul(jnp.matmul(inv_out, example_grad, precision=highest), inv_in, precision=highest)
    flat_train = shaped.reshape(SEQS, KO * KI)
    return jnp.dot(test_grads, flat_train.T, precision=highest)
```

```python
import functools

import jax
import jax.numpy as jnp
from jax import lax
from jax.experimental import pallas as pl
from jax.experimental.pallas import tpu as pltpu
from jax.sharding import PartitionSpec as P

damping = 0.1
HIGHEST = lax.Precision.HIGHEST
F32 = jnp.float32


def dot_nt(a, b, precision=None):
    return lax.dot_general(
        a, b, (((1,), (1,)), ((), ())), precision=precision, preferred_element_type=F32
    )


def dot_nn(a, b):
    return jnp.dot(a, b, precision=HIGHEST, preferred_element_type=F32)


def chunk_of(width):
    for size in (1024, 512, 256, 128):
        if width % size == 0:
            return size
    return width


def twin_inverse(tiles, width):
    wide = tiles[0].shape[1]
    lane = lax.rem(lax.broadcasted_iota(jnp.int32, (8, wide), 1), width)
    row = lax.broadcasted_iota(jnp.int32, (8, wide), 0)
    tiles = list(tiles)
    count = width // 8
    for k in range(count):
        inside = (lane >= 8 * k) & (lane < 8 * k + 8)
        pivots = tiles[k]
        cols = [jnp.broadcast_to(pivots[:, 8 * k + j : 8 * k + j + 1], (8, wide)) for j in range(8)]
        work = jnp.where(inside, (lane - 8 * k == row).astype(F32), pivots)
        for j in range(8):
            scale = 1.0 / cols[j][j : j + 1, :]
            here = row == j
            factor = cols[j]
            line = work[j : j + 1, :] * scale
            work = jnp.where(here, line, work - factor * line)
            for m in range(j + 1, 8):
                line = cols[m][j : j + 1, :] * scale
                cols[m] = jnp.where(here, line, cols[m] - factor * line)
        for i in range(count):
            if i == k:
                continue
            total = jnp.where(inside, 0.0, tiles[i])
            for j in range(8):
                column = jnp.broadcast_to(
                    tiles[i][:, 8 * k + j : 8 * k + j + 1], (8, wide)
                )
                total = total - column * work[j : j + 1, :]
            tiles[i] = total
        tiles[k] = work
    return tiles


def kernel(
    n_dp, n_test,
    lengths_ref, tests_ref, xin_hbm, xout_hbm, pin_hbm, pout_hbm, out_ref,
    xin, xout, pin, pout, gram, sbuf, xbuf, zbuf, gbuf, tmat, inv_own, inv_other,
    load_sem, s_send, s_recv, x_send, x_recv, z_send, z_recv, g_send, g_recv, i_send, i_recv,
):
    dp = lax.axis_index("dp")
    test = lax.axis_index("test")
    core = lax.axis_index("seq")
    half_len, depth_in = xin.shape
    depth_out = xout.shape[1]
    width = pin.shape[0]
    test_local = tests_ref.shape[0]
    wide = 2 * width
    half = width // 2
    pairs = n_test // 2

    partners = [{"seq": 1 - core}]
    partners += [{"test": lax.rem(test + d, n_test)} for d in range(1, n_test)]
    partners += [{"dp": lax.rem(dp + d, n_dp)} for d in range(1, n_dp)]

    barrier = pltpu.get_barrier_semaphore()
    for partner in partners:
        pl.semaphore_signal(barrier, inc=1, device_id=partner, device_id_type=pl.DeviceIdType.MESH)

    loads = []
    plan = []
    for x_hbm, x, p_hbm, p, depth in (
        (xin_hbm, xin, pin_hbm, pin, depth_in),
        (xout_hbm, xout, pout_hbm, pout, depth_out),
    ):
        size = chunk_of(depth)
        steps = []
        for start in range(0, depth, size):
            cut = pl.ds(start, size)
            both = []
            for src, dst in ((x_hbm.at[0, :, cut], x.at[:, cut]), (p_hbm.at[:, cut], p.at[:, cut])):
                copy = pltpu.make_async_copy(src, dst, load_sem.at[len(loads)])
                copy.start()
                loads.append(copy)
                both.append(copy)
            steps.append((start, size, both))
        plan.append((x, p, steps))

    for j in range(test_local):
        for q in range(width * width // wide):
            piece = tests_ref[j : j + 1, q * wide : (q + 1) * wide]
            tmat[j, 2 * q : 2 * q + 1, :] = piece
            tmat[j, 2 * q + 1 : 2 * q + 2, :] = pltpu.roll(piece, width, 1)

    length = lengths_ref[0]
    slots = core * half_len + lax.broadcasted_iota(jnp.int32, (1, half_len), 1)
    valid = (slots < length).astype(F32)
    lows = []
    for x, p, steps in plan:
        total = jnp.zeros((width, half_len), F32)
        for start, size, both in steps:
            for copy in both:
                copy.wait()
            total = total + dot_nt(p[:, start : start + size], x[:, start : start + size])
        lows.append(total * valid)
    low_in, low_out = lows
    own = jnp.where(core == 0, low_in, low_out)
    oth = jnp.where(core == 0, low_out, low_in)

    pl.semaphore_wait(barrier, len(partners))

    gram[...] = dot_nt(oth, jnp.concatenate([oth, own], axis=0), HIGHEST)
    s_copy = pltpu.make_async_remote_copy(
        gram, sbuf, s_send, s_recv, device_id={"seq": 1 - core},
        device_id_type=pl.DeviceIdType.MESH,
    )
    s_copy.start()
    mine = dot_nt(own, jnp.concatenate([own, oth], axis=0), HIGHEST)
    tokens = jnp.clip(length, 0, 2 * half_len).astype(F32)
    xbuf[test, width : width + 8, :] = jnp.full((8, wide), tokens, F32)
    s_copy.wait_recv()
    xbuf[test, 0:width, :] = mine + sbuf[...]

    waits = [s_copy]

    def spread(buffer, me, axis, n, send, recv):
        arrivals = []
        for d in range(1, n):
            copy = pltpu.make_async_remote_copy(
                buffer.at[me], buffer.at[me], send.at[d - 1], recv.at[d - 1],
                device_id={axis: lax.rem(me + d, n)}, device_id_type=pl.DeviceIdType.MESH,
            )
            copy.start()
            waits.append(copy)
            source = lax.rem(me + n - d, n)
            arrivals.append(
                pltpu.make_async_remote_copy(
                    buffer.at[source], buffer.at[source], send.at[d - 1], recv.at[d - 1],
                    device_id={axis: lax.rem(me + d, n)}, device_id_type=pl.DeviceIdType.MESH,
                )
            )
        return arrivals

    for arrival in spread(xbuf, test, "test", n_test, x_send, x_recv):
        arrival.wait_recv()
    lane = lax.broadcasted_iota(jnp.int32, (half, wide), 1)
    left = lane < width
    cov = xbuf[0, 0:width, :]
    for i in range(1, n_test):
        cov = cov + xbuf[i, 0:width, :]
    zbuf[dp] = jnp.where(left, cov[0:half], pltpu.roll(cov[half:width], width, 1))
    z_arrivals = spread(zbuf, dp, "dp", n_dp, z_send, z_recv)
    left_full = lax.broadcasted_iota(jnp.int32, (width, wide), 1) < width
    for i in range(pairs):
        gbuf[dp, i * width : (i + 1) * width, :] = jnp.where(
            left_full,
            pltpu.roll(xbuf[2 * i, 0:width, :], width, 1),
            xbuf[2 * i + 1, 0:width, :],
        )
    amount = xbuf[0, width : width + 8, :]
    for i in range(1, n_test):
        amount = amount + xbuf[i, width : width + 8, :]
    gbuf[dp, pairs * width : pairs * width + 8, :] = amount
    g_arrivals = spread(gbuf, dp, "dp", n_dp, g_send, g_recv)

    for arrival in z_arrivals:
        arrival.wait_recv()
    packed = zbuf[0]
    for i in range(1, n_dp):
        packed = packed + zbuf[i]
    turned = pltpu.roll(packed, width, 1)
    twin = jnp.concatenate(
        [jnp.where(left, packed, turned), jnp.where(left, turned, packed)], axis=0
    )
    eye = lax.broadcasted_iota(jnp.int32, (width, wide), 0) == lax.rem(
        lax.broadcasted_iota(jnp.int32, (width, wide), 1), width
    )
    diagonal = jnp.where(eye, twin, 0.0)
    shift = (damping / width) * (0.5 * jnp.sum(diagonal))
    damped = twin + jnp.where(eye, shift, 0.0)
    tiles = twin_inverse([damped[8 * i : 8 * i + 8] for i in range(width // 8)], width)
    inverse = jnp.concatenate(tiles, axis=0)
    inv_own[...] = inverse
    i_copy = pltpu.make_async_remote_copy(
        inv_own, inv_other, i_send, i_recv, device_id={"seq": 1 - core},
        device_id_type=pl.DeviceIdType.MESH,
    )
    i_copy.start()
    waits.append(i_copy)

    sides = []
    for j in range(test_local):
        matrix = tmat[j][:, 0:width]
        sides.append(dot_nn(inverse[:, 0:width], jnp.where(core == 0, matrix.T, matrix)))
    sides = jnp.concatenate(sides, axis=0)
    for arrival in g_arrivals:
        arrival.wait_recv()
    amount = gbuf[0, pairs * width : pairs * width + 1, :]
    for i in range(1, n_dp):
        amount = amount + gbuf[i, pairs * width : pairs * width + 1, :]
    i_copy.wait_recv()
    scorer = dot_nn(sides, inv_other[...])
    left_row = lax.broadcasted_iota(jnp.int32, (1, wide), 1) < width
    ones = jnp.ones((8, wide), F32)
    for j in range(test_local):
        rows = []
        for z in range(n_dp):
            for i in range(pairs):
                part = jnp.sum(
                    scorer[j * width : (j + 1) * width] * gbuf[z, i * width : (i + 1) * width, :],
                    axis=0, keepdims=True,
                )
                part = part * amount * amount
                rows.append(jnp.where(left_row, part, 0.0))
                rows.append(jnp.where(left_row, 0.0, part))
        result = dot_nt(ones, jnp.concatenate(rows, axis=0), HIGHEST)
        out_ref[j : j + 1, :] = result[0:1, :]

    for copy in waits:
        copy.wait_send()


def per_device(n_dp, n_test, train_inputs, train_grads, lengths, proj_in, proj_out, test_grads):
    _, half_len, depth_in = train_inputs.shape
    depth_out = train_grads.shape[2]
    width = proj_in.shape[0]
    wide = 2 * width
    test_local = test_grads.shape[0]
    bf16 = train_inputs.dtype
    n_loads = 2 * (depth_in // chunk_of(depth_in) + depth_out // chunk_of(depth_out))
    any_space = pl.BlockSpec(memory_space=pl.ANY)
    dma = pltpu.SemaphoreType.DMA
    return pl.pallas_call(
        functools.partial(kernel, n_dp, n_test),
        out_shape=jax.ShapeDtypeStruct((test_local, n_dp * n_test), F32),
        in_specs=[
            pl.BlockSpec(memory_space=pltpu.SMEM),
            pl.BlockSpec(memory_space=pltpu.VMEM),
            any_space, any_space, any_space, any_space,
        ],
        out_specs=pl.BlockSpec(memory_space=pltpu.VMEM),
        scratch_shapes=[
            pltpu.VMEM((half_len, depth_in), bf16),
            pltpu.VMEM((half_len, depth_out), bf16),
            pltpu.VMEM((width, depth_in), bf16),
            pltpu.VMEM((width, depth_out), bf16),
            pltpu.VMEM((width, wide), F32),
            pltpu.VMEM((width, wide), F32),
            pltpu.VMEM((n_test, width + 8, wide), F32),
            pltpu.VMEM((n_dp, width // 2, wide), F32),
            pltpu.VMEM((n_dp, n_test // 2 * width + 8, wide), F32),
            pltpu.VMEM((test_local, width, wide), F32),
            pltpu.VMEM((width, wide), F32),
            pltpu.VMEM((width, wide), F32),
            dma((n_loads,)),
            dma, dma,
            dma((n_test - 1,)), dma((n_test - 1,)),
            dma((n_dp - 1,)), dma((n_dp - 1,)),
            dma((n_dp - 1,)), dma((n_dp - 1,)),
            dma, dma,
        ],
        compiler_params=pltpu.CompilerParams(
            collective_id=0, has_side_effects=True, vmem_limit_bytes=32 * 1024 * 1024
        ),
    )(lengths, test_grads, train_inputs, train_grads, proj_in, proj_out)


def solution(mesh):
    return jax.shard_map(
        functools.partial(per_device, mesh.shape["dp"], mesh.shape["test"]),
        mesh=mesh,
        in_specs=(
            P(("grp", "dp", "test"), "seq", None),
            P(("grp", "dp", "test"), "seq", None),
            P(("grp", "dp", "test")),
            P(),
            P(),
            P(("grp", "dp", "test"), None),
        ),
        out_specs=P(("grp", "dp", "test"), None),
        check_vma=False,
    )
```

```python
import functools

import jax
import jax.numpy as jnp
from jax import lax
from jax.experimental import pallas as pl
from jax.experimental.pallas import tpu as pltpu
from jax.sharding import PartitionSpec as P

damping = 0.1
HIGHEST = lax.Precision.HIGHEST
F32 = jnp.float32


def dot_nt(a, b, precision=None):
    return lax.dot_general(
        a, b, (((1,), (1,)), ((), ())), precision=precision, preferred_element_type=F32
    )


def dot_nn(a, b):
    return jnp.dot(a, b, precision=HIGHEST, preferred_element_type=F32)


def chunk_of(width):
    for size in (1024, 512, 256, 128):
        if width % size == 0:
            return size
    return width


def twin_inverse(tiles, width):
    wide = tiles[0].shape[1]
    lane = lax.rem(lax.broadcasted_iota(jnp.int32, (8, wide), 1), width)
    row = lax.broadcasted_iota(jnp.int32, (8, wide), 0)
    tiles = list(tiles)
    count = width // 8
    for k in range(count):
        inside = (lane >= 8 * k) & (lane < 8 * k + 8)
        pivots = tiles[k]
        cols = [jnp.broadcast_to(pivots[:, 8 * k + j : 8 * k + j + 1], (8, wide)) for j in range(8)]
        work = jnp.where(inside, (lane - 8 * k == row).astype(F32), pivots)
        for j in range(8):
            scale = 1.0 / cols[j][j : j + 1, :]
            here = row == j
            factor = cols[j]
            line = work[j : j + 1, :] * scale
            work = jnp.where(here, line, work - factor * line)
            for m in range(j + 1, 8):
                line = cols[m][j : j + 1, :] * scale
                cols[m] = jnp.where(here, line, cols[m] - factor * line)
        for i in range(count):
            if i == k:
                continue
            total = jnp.where(inside, 0.0, tiles[i])
            for j in range(8):
                column = jnp.broadcast_to(
                    tiles[i][:, 8 * k + j : 8 * k + j + 1], (8, wide)
                )
                total = total - column * work[j : j + 1, :]
            tiles[i] = total
        tiles[k] = work
    return tiles


def kernel(
    n_dp, n_test,
    lengths_ref, tests_hbm, xin_hbm, xout_hbm, pin_hbm, pout_hbm, out_ref,
    tests_ref, xin, xout, pin, pout, gram, sbuf, xbuf, zbuf, gbuf, tmat, inv_own, inv_other,
    load_sem, small_sem, s_send, s_recv, x_send, x_recv, z_send, z_recv, g_send, g_recv, i_send, i_recv,
):
    dp = lax.axis_index("dp")
    test = lax.axis_index("test")
    core = lax.axis_index("seq")
    half_len, depth_in = xin.shape
    depth_out = xout.shape[1]
    width = pin.shape[0]
    test_local = tests_ref.shape[0]
    wide = 2 * width
    half = width // 2
    pairs = n_test // 2

    partners = [{"seq": 1 - core}]
    partners += [{"test": lax.rem(test + d, n_test)} for d in range(1, n_test)]
    partners += [{"dp": lax.rem(dp + d, n_dp)} for d in range(1, n_dp)]

    barrier = pltpu.get_barrier_semaphore()
    for partner in partners:
        pl.semaphore_signal(barrier, inc=1, device_id=partner, device_id_type=pl.DeviceIdType.MESH)

    loads = []
    plan = []
    for x_hbm, x, p_hbm, p, depth in (
        (xin_hbm, xin, pin_hbm, pin, depth_in),
        (xout_hbm, xout, pout_hbm, pout, depth_out),
    ):
        size = chunk_of(depth)
        steps = []
        for start in range(0, depth, size):
            cut = pl.ds(start, size)
            both = []
            for src, dst in ((x_hbm.at[0, :, cut], x.at[:, cut]), (p_hbm.at[:, cut], p.at[:, cut])):
                copy = pltpu.make_async_copy(src, dst, load_sem.at[len(loads)])
                copy.start()
                loads.append(copy)
                both.append(copy)
            steps.append((start, size, both))
        plan.append((x, p, steps))

    tests_copy = pltpu.make_async_copy(tests_hbm, tests_ref, small_sem)
    tests_copy.start()

    length = lengths_ref[0]
    slots = core * half_len + lax.broadcasted_iota(jnp.int32, (1, half_len), 1)
    valid = (slots < length).astype(F32)
    lows = []
    for x, p, steps in plan:
        total = jnp.zeros((width, half_len), F32)
        for start, size, both in steps:
            for copy in both:
                copy.wait()
            total = total + dot_nt(p[:, start : start + size], x[:, start : start + size])
        lows.append(total * valid)
    low_in, low_out = lows
    own = jnp.where(core == 0, low_in, low_out)
    oth = jnp.where(core == 0, low_out, low_in)

    pl.semaphore_wait(barrier, len(partners))

    gram[...] = dot_nt(oth, jnp.concatenate([oth, own], axis=0), HIGHEST)
    s_copy = pltpu.make_async_remote_copy(
        gram, sbuf, s_send, s_recv, device_id={"seq": 1 - core},
        device_id_type=pl.DeviceIdType.MESH,
    )
    s_copy.start()
    mine = dot_nt(own, jnp.concatenate([own, oth], axis=0), HIGHEST)
    tokens = jnp.clip(length, 0, 2 * half_len).astype(F32)
    xbuf[test, width : width + 8, :] = jnp.full((8, wide), tokens, F32)
    s_copy.wait_recv()
    xbuf[test, 0:width, :] = mine + sbuf[...]

    waits = [s_copy]

    def spread(buffer, me, axis, n, send, recv):
        arrivals = []
        for d in range(1, n):
            copy = pltpu.make_async_remote_copy(
                buffer.at[me], buffer.at[me], send.at[d - 1], recv.at[d - 1],
                device_id={axis: lax.rem(me + d, n)}, device_id_type=pl.DeviceIdType.MESH,
            )
            copy.start()
            waits.append(copy)
            source = lax.rem(me + n - d, n)
            arrivals.append(
                pltpu.make_async_remote_copy(
                    buffer.at[source], buffer.at[source], send.at[d - 1], recv.at[d - 1],
                    device_id={axis: lax.rem(me + d, n)}, device_id_type=pl.DeviceIdType.MESH,
                )
            )
        return arrivals

    for arrival in spread(xbuf, test, "test", n_test, x_send, x_recv):
        arrival.wait_recv()
    lane = lax.broadcasted_iota(jnp.int32, (half, wide), 1)
    left = lane < width
    cov = xbuf[0, 0:width, :]
    for i in range(1, n_test):
        cov = cov + xbuf[i, 0:width, :]
    zbuf[dp] = jnp.where(left, cov[0:half], pltpu.roll(cov[half:width], width, 1))
    z_arrivals = spread(zbuf, dp, "dp", n_dp, z_send, z_recv)
    left_full = lax.broadcasted_iota(jnp.int32, (width, wide), 1) < width
    for i in range(pairs):
        gbuf[dp, i * width : (i + 1) * width, :] = jnp.where(
            left_full,
            pltpu.roll(xbuf[2 * i, 0:width, :], width, 1),
            xbuf[2 * i + 1, 0:width, :],
        )
    amount = xbuf[0, width : width + 8, :]
    for i in range(1, n_test):
        amount = amount + xbuf[i, width : width + 8, :]
    gbuf[dp, pairs * width : pairs * width + 8, :] = amount
    g_arrivals = spread(gbuf, dp, "dp", n_dp, g_send, g_recv)

    tests_copy.wait()
    for j in range(test_local):
        for q in range(width * width // wide):
            piece = tests_ref[j : j + 1, q * wide : (q + 1) * wide]
            tmat[j, 2 * q : 2 * q + 1, :] = piece
            tmat[j, 2 * q + 1 : 2 * q + 2, :] = pltpu.roll(piece, width, 1)

    for arrival in z_arrivals:
        arrival.wait_recv()
    packed = zbuf[0]
    for i in range(1, n_dp):
        packed = packed + zbuf[i]
    turned = pltpu.roll(packed, width, 1)
    twin = jnp.concatenate(
        [jnp.where(left, packed, turned), jnp.where(left, turned, packed)], axis=0
    )
    eye = lax.broadcasted_iota(jnp.int32, (width, wide), 0) == lax.rem(
        lax.broadcasted_iota(jnp.int32, (width, wide), 1), width
    )
    diagonal = jnp.where(eye, twin, 0.0)
    shift = (damping / width) * (0.5 * jnp.sum(diagonal))
    damped = twin + jnp.where(eye, shift, 0.0)
    tiles = twin_inverse([damped[8 * i : 8 * i + 8] for i in range(width // 8)], width)
    inverse = jnp.concatenate(tiles, axis=0)
    inv_own[...] = inverse
    i_copy = pltpu.make_async_remote_copy(
        inv_own, inv_other, i_send, i_recv, device_id={"seq": 1 - core},
        device_id_type=pl.DeviceIdType.MESH,
    )
    i_copy.start()
    waits.append(i_copy)

    sides = []
    for j in range(test_local):
        matrix = tmat[j][:, 0:width]
        sides.append(dot_nn(inverse[:, 0:width], jnp.where(core == 0, matrix.T, matrix)))
    sides = jnp.concatenate(sides, axis=0)
    for arrival in g_arrivals:
        arrival.wait_recv()
    amount = gbuf[0, pairs * width : pairs * width + 1, :]
    for i in range(1, n_dp):
        amount = amount + gbuf[i, pairs * width : pairs * width + 1, :]
    i_copy.wait_recv()
    scorer = dot_nn(sides, inv_other[...])
    left_row = lax.broadcasted_iota(jnp.int32, (1, wide), 1) < width
    ones = jnp.ones((8, wide), F32)
    for j in range(test_local):
        rows = []
        for z in range(n_dp):
            for i in range(pairs):
                part = jnp.sum(
                    scorer[j * width : (j + 1) * width] * gbuf[z, i * width : (i + 1) * width, :],
                    axis=0, keepdims=True,
                )
                part = part * amount * amount
                rows.append(jnp.where(left_row, part, 0.0))
                rows.append(jnp.where(left_row, 0.0, part))
        result = dot_nt(ones, jnp.concatenate(rows, axis=0), HIGHEST)
        out_ref[j : j + 1, :] = result[0:1, :]

    for copy in waits:
        copy.wait_send()


def per_device(n_dp, n_test, train_inputs, train_grads, lengths, proj_in, proj_out, test_grads):
    _, half_len, depth_in = train_inputs.shape
    depth_out = train_grads.shape[2]
    width = proj_in.shape[0]
    wide = 2 * width
    test_local = test_grads.shape[0]
    bf16 = train_inputs.dtype
    n_loads = 2 * (depth_in // chunk_of(depth_in) + depth_out // chunk_of(depth_out))
    any_space = pl.BlockSpec(memory_space=pltpu.HBM)
    dma = pltpu.SemaphoreType.DMA
    return pl.pallas_call(
        functools.partial(kernel, n_dp, n_test),
        out_shape=jax.ShapeDtypeStruct((test_local, n_dp * n_test), F32),
        in_specs=[
            pl.BlockSpec(memory_space=pltpu.SMEM),
            any_space, any_space, any_space, any_space, any_space,
        ],
        out_specs=pl.BlockSpec(memory_space=pltpu.VMEM),
        scratch_shapes=[
            pltpu.VMEM(test_grads.shape, F32),
            pltpu.VMEM((half_len, depth_in), bf16),
            pltpu.VMEM((half_len, depth_out), bf16),
            pltpu.VMEM((width, depth_in), bf16),
            pltpu.VMEM((width, depth_out), bf16),
            pltpu.VMEM((width, wide), F32),
            pltpu.VMEM((width, wide), F32),
            pltpu.VMEM((n_test, width + 8, wide), F32),
            pltpu.VMEM((n_dp, width // 2, wide), F32),
            pltpu.VMEM((n_dp, n_test // 2 * width + 8, wide), F32),
            pltpu.VMEM((test_local, width, wide), F32),
            pltpu.VMEM((width, wide), F32),
            pltpu.VMEM((width, wide), F32),
            dma((n_loads,)),
            dma,
            dma, dma,
            dma((n_test - 1,)), dma((n_test - 1,)),
            dma((n_dp - 1,)), dma((n_dp - 1,)),
            dma((n_dp - 1,)), dma((n_dp - 1,)),
            dma, dma,
        ],
        compiler_params=pltpu.CompilerParams(
            collective_id=0, has_side_effects=True, vmem_limit_bytes=60 * 1024 * 1024
        ),
    )(lengths, test_grads, train_inputs, train_grads, proj_in, proj_out)


def solution(mesh):
    return jax.shard_map(
        functools.partial(per_device, mesh.shape["dp"], mesh.shape["test"]),
        mesh=mesh,
        in_specs=(
            P(("grp", "dp", "test"), "seq", None),
            P(("grp", "dp", "test"), "seq", None),
            P(("grp", "dp", "test")),
            P(),
            P(),
            P(("grp", "dp", "test"), None),
        ),
        out_specs=P(("grp", "dp", "test"), None),
        check_vma=False,
    )
```

```python
import functools

import jax
import jax.numpy as jnp
from jax import lax
from jax.experimental import pallas as pl
from jax.experimental.pallas import tpu as pltpu
from jax.sharding import PartitionSpec as P

damping = 0.1
HIGHEST = lax.Precision.HIGHEST
F32 = jnp.float32


def dot_nt(a, b, precision=None):
    return lax.dot_general(
        a, b, (((1,), (1,)), ((), ())), precision=precision, preferred_element_type=F32
    )


def dot_nn(a, b):
    return jnp.dot(a, b, precision=HIGHEST, preferred_element_type=F32)


def chunk_of(width):
    for size in (1024, 512, 256, 128):
        if width % size == 0:
            return size
    return width


def twin_inverse(tiles, width):
    wide = tiles[0].shape[1]
    lane = lax.rem(lax.broadcasted_iota(jnp.int32, (8, wide), 1), width)
    row = lax.broadcasted_iota(jnp.int32, (8, wide), 0)
    tiles = list(tiles)
    count = width // 8
    for k in range(count):
        inside = (lane >= 8 * k) & (lane < 8 * k + 8)
        pivots = tiles[k]
        cols = [jnp.broadcast_to(pivots[:, 8 * k + j : 8 * k + j + 1], (8, wide)) for j in range(8)]
        work = jnp.where(inside, (lane - 8 * k == row).astype(F32), pivots)
        for j in range(8):
            scale = 1.0 / cols[j][j : j + 1, :]
            here = row == j
            factor = cols[j]
            line = work[j : j + 1, :] * scale
            work = jnp.where(here, line, work - factor * line)
            for m in range(j + 1, 8):
                line = cols[m][j : j + 1, :] * scale
                cols[m] = jnp.where(here, line, cols[m] - factor * line)
        for i in range(count):
            if i == k:
                continue
            total = jnp.where(inside, 0.0, tiles[i])
            for j in range(8):
                column = jnp.broadcast_to(
                    tiles[i][:, 8 * k + j : 8 * k + j + 1], (8, wide)
                )
                total = total - column * work[j : j + 1, :]
            tiles[i] = total
        tiles[k] = work
    return tiles


def kernel(
    n_dp, n_test,
    lengths_hbm, tests_hbm, xin_hbm, xout_hbm, pin_hbm, pout_hbm, out_ref,
    lengths_ref, tests_ref, xin, xout, pin, pout, gram, sbuf, xbuf, zbuf, gbuf, tmat, inv_own, inv_other,
    load_sem, small_sem, s_send, s_recv, x_send, x_recv, z_send, z_recv, g_send, g_recv, i_send, i_recv,
):
    dp = lax.axis_index("dp")
    test = lax.axis_index("test")
    core = lax.axis_index("seq")
    half_len, depth_in = xin.shape
    depth_out = xout.shape[1]
    width = pin.shape[0]
    test_local = tests_ref.shape[0]
    wide = 2 * width
    half = width // 2
    pairs = n_test // 2

    partners = [{"seq": 1 - core}]
    partners += [{"test": lax.rem(test + d, n_test)} for d in range(1, n_test)]
    partners += [{"dp": lax.rem(dp + d, n_dp)} for d in range(1, n_dp)]

    barrier = pltpu.get_barrier_semaphore()
    for partner in partners:
        pl.semaphore_signal(barrier, inc=1, device_id=partner, device_id_type=pl.DeviceIdType.MESH)

    loads = []
    plan = []
    for x_hbm, x, p_hbm, p, depth in (
        (xin_hbm, xin, pin_hbm, pin, depth_in),
        (xout_hbm, xout, pout_hbm, pout, depth_out),
    ):
        size = chunk_of(depth)
        steps = []
        for start in range(0, depth, size):
            cut = pl.ds(start, size)
            both = []
            for src, dst in ((x_hbm.at[0, :, cut], x.at[:, cut]), (p_hbm.at[:, cut], p.at[:, cut])):
                copy = pltpu.make_async_copy(src, dst, load_sem.at[len(loads)])
                copy.start()
                loads.append(copy)
                both.append(copy)
            steps.append((start, size, both))
        plan.append((x, p, steps))

    length_copy = pltpu.make_async_copy(lengths_hbm, lengths_ref, small_sem.at[0])
    length_copy.start()
    tests_copy = pltpu.make_async_copy(tests_hbm, tests_ref, small_sem.at[1])
    tests_copy.start()

    length_copy.wait()
    length = lengths_ref[...]
    slots = core * half_len + lax.broadcasted_iota(jnp.int32, (1, half_len), 1)
    valid = (slots < length).astype(F32)
    lows = []
    for x, p, steps in plan:
        total = jnp.zeros((width, half_len), F32)
        for start, size, both in steps:
            for copy in both:
                copy.wait()
            total = total + dot_nt(p[:, start : start + size], x[:, start : start + size])
        lows.append(total * valid)
    low_in, low_out = lows
    own = jnp.where(core == 0, low_in, low_out)
    oth = jnp.where(core == 0, low_out, low_in)

    pl.semaphore_wait(barrier, len(partners))

    gram[...] = dot_nt(oth, jnp.concatenate([oth, own], axis=0), HIGHEST)
    s_copy = pltpu.make_async_remote_copy(
        gram, sbuf, s_send, s_recv, device_id={"seq": 1 - core},
        device_id_type=pl.DeviceIdType.MESH,
    )
    s_copy.start()
    mine = dot_nt(own, jnp.concatenate([own, oth], axis=0), HIGHEST)
    tokens = jnp.clip(length, 0, 2 * half_len).astype(F32)
    xbuf[test, width : width + 8, :] = jnp.broadcast_to(tokens, (8, wide))
    s_copy.wait_recv()
    xbuf[test, 0:width, :] = mine + sbuf[...]

    waits = [s_copy]

    def spread(buffer, me, axis, n, send, recv):
        arrivals = []
        for d in range(1, n):
            copy = pltpu.make_async_remote_copy(
                buffer.at[me], buffer.at[me], send.at[d - 1], recv.at[d - 1],
                device_id={axis: lax.rem(me + d, n)}, device_id_type=pl.DeviceIdType.MESH,
            )
            copy.start()
            waits.append(copy)
            source = lax.rem(me + n - d, n)
            arrivals.append(
                pltpu.make_async_remote_copy(
                    buffer.at[source], buffer.at[source], send.at[d - 1], recv.at[d - 1],
                    device_id={axis: lax.rem(me + d, n)}, device_id_type=pl.DeviceIdType.MESH,
                )
            )
        return arrivals

    for arrival in spread(xbuf, test, "test", n_test, x_send, x_recv):
        arrival.wait_recv()
    lane = lax.broadcasted_iota(jnp.int32, (half, wide), 1)
    left = lane < width
    cov = xbuf[0, 0:width, :]
    for i in range(1, n_test):
        cov = cov + xbuf[i, 0:width, :]
    zbuf[dp] = jnp.where(left, cov[0:half], pltpu.roll(cov[half:width], width, 1))
    z_arrivals = spread(zbuf, dp, "dp", n_dp, z_send, z_recv)
    left_full = lax.broadcasted_iota(jnp.int32, (width, wide), 1) < width
    for i in range(pairs):
        gbuf[dp, i * width : (i + 1) * width, :] = jnp.where(
            left_full,
            pltpu.roll(xbuf[2 * i, 0:width, :], width, 1),
            xbuf[2 * i + 1, 0:width, :],
        )
    amount = xbuf[0, width : width + 8, :]
    for i in range(1, n_test):
        amount = amount + xbuf[i, width : width + 8, :]
    gbuf[dp, pairs * width : pairs * width + 8, :] = amount
    g_arrivals = spread(gbuf, dp, "dp", n_dp, g_send, g_recv)

    tests_copy.wait()
    for j in range(test_local):
        for q in range(width * width // wide):
            piece = tests_ref[j : j + 1, q * wide : (q + 1) * wide]
            tmat[j, 2 * q : 2 * q + 1, :] = piece
            tmat[j, 2 * q + 1 : 2 * q + 2, :] = pltpu.roll(piece, width, 1)

    for arrival in z_arrivals:
        arrival.wait_recv()
    packed = zbuf[0]
    for i in range(1, n_dp):
        packed = packed + zbuf[i]
    turned = pltpu.roll(packed, width, 1)
    twin = jnp.concatenate(
        [jnp.where(left, packed, turned), jnp.where(left, turned, packed)], axis=0
    )
    eye = lax.broadcasted_iota(jnp.int32, (width, wide), 0) == lax.rem(
        lax.broadcasted_iota(jnp.int32, (width, wide), 1), width
    )
    diagonal = jnp.where(eye, twin, 0.0)
    shift = (damping / width) * (0.5 * jnp.sum(diagonal))
    damped = twin + jnp.where(eye, shift, 0.0)
    tiles = twin_inverse([damped[8 * i : 8 * i + 8] for i in range(width // 8)], width)
    inverse = jnp.concatenate(tiles, axis=0)
    inv_own[...] = inverse
    i_copy = pltpu.make_async_remote_copy(
        inv_own, inv_other, i_send, i_recv, device_id={"seq": 1 - core},
        device_id_type=pl.DeviceIdType.MESH,
    )
    i_copy.start()
    waits.append(i_copy)

    sides = []
    for j in range(test_local):
        matrix = tmat[j][:, 0:width]
        sides.append(dot_nn(inverse[:, 0:width], jnp.where(core == 0, matrix.T, matrix)))
    sides = jnp.concatenate(sides, axis=0)
    for arrival in g_arrivals:
        arrival.wait_recv()
    amount = gbuf[0, pairs * width : pairs * width + 1, :]
    for i in range(1, n_dp):
        amount = amount + gbuf[i, pairs * width : pairs * width + 1, :]
    i_copy.wait_recv()
    scorer = dot_nn(sides, inv_other[...])
    left_row = lax.broadcasted_iota(jnp.int32, (1, wide), 1) < width
    ones = jnp.ones((8, wide), F32)
    for j in range(test_local):
        rows = []
        for z in range(n_dp):
            for i in range(pairs):
                part = jnp.sum(
                    scorer[j * width : (j + 1) * width] * gbuf[z, i * width : (i + 1) * width, :],
                    axis=0, keepdims=True,
                )
                part = part * amount * amount
                rows.append(jnp.where(left_row, part, 0.0))
                rows.append(jnp.where(left_row, 0.0, part))
        result = dot_nt(ones, jnp.concatenate(rows, axis=0), HIGHEST)
        out_ref[j : j + 1, :] = result[0:1, :]

    for copy in waits:
        copy.wait_send()


def per_device(n_dp, n_test, train_inputs, train_grads, lengths, proj_in, proj_out, test_grads):
    _, half_len, depth_in = train_inputs.shape
    depth_out = train_grads.shape[2]
    width = proj_in.shape[0]
    wide = 2 * width
    test_local = test_grads.shape[0]
    bf16 = train_inputs.dtype
    n_loads = 2 * (depth_in // chunk_of(depth_in) + depth_out // chunk_of(depth_out))
    any_space = pl.BlockSpec(memory_space=pltpu.HBM)
    dma = pltpu.SemaphoreType.DMA
    return pl.pallas_call(
        functools.partial(kernel, n_dp, n_test),
        out_shape=jax.ShapeDtypeStruct((test_local, n_dp * n_test), F32),
        in_specs=[
            any_space, any_space, any_space, any_space, any_space, any_space,
        ],
        out_specs=pl.BlockSpec(memory_space=pltpu.VMEM),
        scratch_shapes=[
            pltpu.VMEM((1, 1), jnp.int32),
            pltpu.VMEM(test_grads.shape, F32),
            pltpu.VMEM((half_len, depth_in), bf16),
            pltpu.VMEM((half_len, depth_out), bf16),
            pltpu.VMEM((width, depth_in), bf16),
            pltpu.VMEM((width, depth_out), bf16),
            pltpu.VMEM((width, wide), F32),
            pltpu.VMEM((width, wide), F32),
            pltpu.VMEM((n_test, width + 8, wide), F32),
            pltpu.VMEM((n_dp, width // 2, wide), F32),
            pltpu.VMEM((n_dp, n_test // 2 * width + 8, wide), F32),
            pltpu.VMEM((test_local, width, wide), F32),
            pltpu.VMEM((width, wide), F32),
            pltpu.VMEM((width, wide), F32),
            dma((n_loads,)),
            dma((2,)),
            dma, dma,
            dma((n_test - 1,)), dma((n_test - 1,)),
            dma((n_dp - 1,)), dma((n_dp - 1,)),
            dma((n_dp - 1,)), dma((n_dp - 1,)),
            dma, dma,
        ],
        compiler_params=pltpu.CompilerParams(
            collective_id=0, has_side_effects=True, vmem_limit_bytes=55200 * 1024
        ),
    )(lengths.reshape(1, 1), test_grads, train_inputs, train_grads, proj_in, proj_out)


def solution(mesh):
    return jax.shard_map(
        functools.partial(per_device, mesh.shape["dp"], mesh.shape["test"]),
        mesh=mesh,
        in_specs=(
            P(("grp", "dp", "test"), "seq", None),
            P(("grp", "dp", "test"), "seq", None),
            P(("grp", "dp", "test")),
            P(),
            P(),
            P(("grp", "dp", "test"), None),
        ),
        out_specs=P(("grp", "dp", "test"), None),
        check_vma=False,
    )
```

```python
import functools

import jax
import jax.numpy as jnp
from jax import lax
from jax.experimental import pallas as pl
from jax.experimental.pallas import tpu as pltpu
from jax.sharding import PartitionSpec as P

damping = 0.1
HIGHEST = lax.Precision.HIGHEST
F32 = jnp.float32


def dot_nt(a, b, precision=None):
    return lax.dot_general(
        a, b, (((1,), (1,)), ((), ())), precision=precision, preferred_element_type=F32
    )


def dot_nn(a, b):
    return jnp.dot(a, b, precision=HIGHEST, preferred_element_type=F32)


def chunk_of(width):
    for size in (1024, 512, 256, 128):
        if width % size == 0:
            return size
    return width


def twin_inverse(tiles, width):
    wide = tiles[0].shape[1]
    lane = lax.rem(lax.broadcasted_iota(jnp.int32, (8, wide), 1), width)
    row = lax.broadcasted_iota(jnp.int32, (8, wide), 0)
    tiles = list(tiles)
    count = width // 8
    for k in range(count):
        inside = (lane >= 8 * k) & (lane < 8 * k + 8)
        pivots = tiles[k]
        cols = [jnp.broadcast_to(pivots[:, 8 * k + j : 8 * k + j + 1], (8, wide)) for j in range(8)]
        work = jnp.where(inside, (lane - 8 * k == row).astype(F32), pivots)
        for j in range(8):
            scale = 1.0 / cols[j][j : j + 1, :]
            here = row == j
            factor = cols[j]
            line = work[j : j + 1, :] * scale
            work = jnp.where(here, line, work - factor * line)
            for m in range(j + 1, 8):
                line = cols[m][j : j + 1, :] * scale
                cols[m] = jnp.where(here, line, cols[m] - factor * line)
        for i in range(count):
            if i == k:
                continue
            total = jnp.where(inside, 0.0, tiles[i])
            for j in range(8):
                column = jnp.broadcast_to(
                    tiles[i][:, 8 * k + j : 8 * k + j + 1], (8, wide)
                )
                total = total - column * work[j : j + 1, :]
            tiles[i] = total
        tiles[k] = work
    return tiles


def kernel(
    n_dp, n_test,
    lengths_hbm, tests_hbm, xin_hbm, xout_hbm, pin_hbm, pout_hbm, out_ref,
    lengths_ref, tests_ref, xin, xout, pin, pout, obuf, ebuf, sbuf, pbuf, zbuf, gbuf, tmat, inv_own, inv_other,
    load_sem, small_sem, p_send, p_recv, s_send, s_recv, x_send, x_recv, z_send, z_recv, g_send, g_recv, i_send, i_recv,
):
    dp = lax.axis_index("dp")
    test = lax.axis_index("test")
    core = lax.axis_index("seq")
    half_len, depth_in = xin.shape
    depth_out = xout.shape[1]
    width = pin.shape[0]
    test_local = tests_ref.shape[0]
    wide = 2 * width
    half = width // 2

    partners = [{"seq": 1 - core}]
    for d in range(1, n_test):
        partners.append({"test": lax.rem(test + d, n_test)})
        partners.append({"test": lax.rem(test + d, n_test), "seq": 1 - core})
    partners += [{"dp": lax.rem(dp + d, n_dp)} for d in range(1, n_dp)]

    barrier = pltpu.get_barrier_semaphore()
    for partner in partners:
        pl.semaphore_signal(barrier, inc=1, device_id=partner, device_id_type=pl.DeviceIdType.MESH)

    loads = []
    plan = []
    for x_hbm, x, p_hbm, p, depth in (
        (xin_hbm, xin, pin_hbm, pin, depth_in),
        (xout_hbm, xout, pout_hbm, pout, depth_out),
    ):
        size = chunk_of(depth)
        steps = []
        for start in range(0, depth, size):
            cut = pl.ds(start, size)
            both = []
            for src, dst in ((x_hbm.at[0, :, cut], x.at[:, cut]), (p_hbm.at[:, cut], p.at[:, cut])):
                copy = pltpu.make_async_copy(src, dst, load_sem.at[len(loads)])
                copy.start()
                loads.append(copy)
                both.append(copy)
            steps.append((start, size, both))
        plan.append((x, p, steps))

    length_copy = pltpu.make_async_copy(lengths_hbm, lengths_ref, small_sem.at[0])
    length_copy.start()
    tests_copy = pltpu.make_async_copy(tests_hbm, tests_ref, small_sem.at[1])
    tests_copy.start()

    length_copy.wait()
    length = lengths_ref[...]
    slots = core * half_len + lax.broadcasted_iota(jnp.int32, (1, half_len), 1)
    valid = (slots < length).astype(F32)
    lows = []
    for x, p, steps in plan:
        total = jnp.zeros((width, half_len), F32)
        for start, size, both in steps:
            for copy in both:
                copy.wait()
            total = total + dot_nt(p[:, start : start + size], x[:, start : start + size])
        lows.append(total * valid)
    low_in, low_out = lows
    own = jnp.where(core == 0, low_in, low_out)
    oth = jnp.where(core == 0, low_out, low_in)

    pl.semaphore_wait(barrier, len(partners))

    left = lax.broadcasted_iota(jnp.int32, (half, wide), 1) < width

    def twice(a, b):
        return dot_nt(a, jnp.concatenate([b, b], axis=0), HIGHEST)

    def pack(twin):
        return jnp.where(left, twin[0:half], twin[half:width])

    waits = []

    def remote(src, dst, send, recv, where, start=True):
        copy = pltpu.make_async_remote_copy(
            src, dst, send, recv, device_id=where, device_id_type=pl.DeviceIdType.MESH
        )
        if start:
            copy.start()
            waits.append(copy)
        return copy

    other = 1 - core
    obuf[...] = pack(twice(oth, oth))
    part_arrivals = []

    def send_part(d, flip):
        to = lax.rem(test + d, n_test)
        source = lax.rem(test + n_test - d, n_test)
        where = {"test": to, "seq": other if flip else core}
        slot = pbuf.at[core, test]
        sems = (p_send.at[flip, d], p_recv.at[flip, d])
        remote(obuf if flip else slot, slot, *sems, where)
        arrived = pbuf.at[other if flip else core, source]
        part_arrivals.append(remote(arrived, arrived, *sems, where, start=False))

    for d in range(n_test - 1, -1, -1):
        send_part(d, 1)
    pbuf[core, test] = pack(twice(own, own))
    for d in range(n_test - 1, 0, -1):
        send_part(d, 0)

    ebuf[...] = pack(twice(oth, own))
    e_copy = remote(ebuf, sbuf, s_send, s_recv, {"seq": other})
    cross = pack(twice(own, oth))
    tokens = jnp.clip(length, 0, 2 * half_len).astype(F32)
    gbuf[dp, test, half : half + 8, :] = jnp.broadcast_to(tokens, (8, wide))
    e_copy.wait_recv()
    gbuf[dp, test, 0:half, :] = cross + sbuf[...]

    test_arrivals = []
    for d in range(1, n_test):
        where = {"test": lax.rem(test + d, n_test)}
        sems = (x_send.at[d - 1], x_recv.at[d - 1])
        remote(gbuf.at[dp, test], gbuf.at[dp, test], *sems, where)
        arrived = gbuf.at[dp, lax.rem(test + n_test - d, n_test)]
        test_arrivals.append(remote(arrived, arrived, *sems, where, start=False))
    g_arrivals = []

    def send_along(t, d):
        at = lax.rem(test + n_test - t, n_test)
        where = {"dp": lax.rem(dp + d, n_dp)}
        sems = (g_send.at[t, d - 1], g_recv.at[t, d - 1])
        remote(gbuf.at[dp, at], gbuf.at[dp, at], *sems, where)
        arrived = gbuf.at[lax.rem(dp + n_dp - d, n_dp), at]
        g_arrivals.append(remote(arrived, arrived, *sems, where, start=False))

    for d in range(1, n_dp):
        send_along(0, d)

    for arrival in part_arrivals:
        arrival.wait_recv()
    cov = None
    for c in range(2):
        for t in range(n_test):
            cov = pbuf[c, t] if cov is None else cov + pbuf[c, t]
    zbuf[dp] = cov
    z_arrivals = []
    for d in range(1, n_dp):
        where = {"dp": lax.rem(dp + d, n_dp)}
        sems = (z_send.at[d - 1], z_recv.at[d - 1])
        remote(zbuf.at[dp], zbuf.at[dp], *sems, where)
        arrived = zbuf.at[lax.rem(dp + n_dp - d, n_dp)]
        z_arrivals.append(remote(arrived, arrived, *sems, where, start=False))
    for t in range(1, n_test):
        test_arrivals[t - 1].wait_recv()
        for d in range(1, n_dp):
            send_along(t, d)

    tests_copy.wait()
    for j in range(test_local):
        for q in range(width * width // wide):
            piece = tests_ref[j : j + 1, q * wide : (q + 1) * wide]
            tmat[j, 2 * q : 2 * q + 1, :] = piece
            tmat[j, 2 * q + 1 : 2 * q + 2, :] = pltpu.roll(piece, width, 1)

    for arrival in z_arrivals:
        arrival.wait_recv()
    packed = zbuf[0]
    for i in range(1, n_dp):
        packed = packed + zbuf[i]
    turned = pltpu.roll(packed, width, 1)
    twin = jnp.concatenate(
        [jnp.where(left, packed, turned), jnp.where(left, turned, packed)], axis=0
    )
    eye = lax.broadcasted_iota(jnp.int32, (width, wide), 0) == lax.rem(
        lax.broadcasted_iota(jnp.int32, (width, wide), 1), width
    )
    diagonal = jnp.where(eye, twin, 0.0)
    shift = (damping / width) * (0.5 * jnp.sum(diagonal))
    damped = twin + jnp.where(eye, shift, 0.0)
    tiles = twin_inverse([damped[8 * i : 8 * i + 8] for i in range(width // 8)], width)
    inverse = jnp.concatenate(tiles, axis=0)
    inv_own[...] = inverse
    i_copy = remote(inv_own, inv_other, i_send, i_recv, {"seq": other})

    sides = []
    for j in range(test_local):
        matrix = tmat[j][:, 0:width]
        sides.append(dot_nn(inverse[:, 0:width], jnp.where(core == 0, matrix.T, matrix)))
    sides = jnp.concatenate(sides, axis=0)
    for arrival in g_arrivals:
        arrival.wait_recv()
    amount = None
    for z in range(n_dp):
        for t in range(n_test):
            more = gbuf[z, t, half : half + 1, :]
            amount = more if amount is None else amount + more
    amount = amount * amount
    i_copy.wait_recv()
    scorer = dot_nn(sides, inv_other[...])
    ones = jnp.ones((8, wide), F32)
    for j in range(test_local):
        packed = pack(scorer[j * width : (j + 1) * width])
        rows = []
        for z in range(n_dp):
            for t in range(n_test):
                rows.append(jnp.sum(packed * gbuf[z, t, 0:half, :], axis=0, keepdims=True) * amount)
        result = dot_nt(ones, jnp.concatenate(rows, axis=0), HIGHEST)
        out_ref[j : j + 1, :] = result[0:1, :]

    for copy in waits:
        copy.wait_send()


def per_device(n_dp, n_test, train_inputs, train_grads, lengths, proj_in, proj_out, test_grads):
    _, half_len, depth_in = train_inputs.shape
    depth_out = train_grads.shape[2]
    width = proj_in.shape[0]
    wide, half = 2 * width, width // 2
    test_local = test_grads.shape[0]
    bf16 = train_inputs.dtype
    n_loads = 2 * (depth_in // chunk_of(depth_in) + depth_out // chunk_of(depth_out))
    any_space = pl.BlockSpec(memory_space=pltpu.HBM)
    dma = pltpu.SemaphoreType.DMA
    return pl.pallas_call(
        functools.partial(kernel, n_dp, n_test),
        out_shape=jax.ShapeDtypeStruct((test_local, n_dp * n_test), F32),
        in_specs=[
            any_space, any_space, any_space, any_space, any_space, any_space,
        ],
        out_specs=pl.BlockSpec(memory_space=pltpu.VMEM),
        scratch_shapes=[
            pltpu.VMEM((1, 1), jnp.int32),
            pltpu.VMEM(test_grads.shape, F32),
            pltpu.VMEM((half_len, depth_in), bf16),
            pltpu.VMEM((half_len, depth_out), bf16),
            pltpu.VMEM((width, depth_in), bf16),
            pltpu.VMEM((width, depth_out), bf16),
            pltpu.VMEM((half, wide), F32),
            pltpu.VMEM((half, wide), F32),
            pltpu.VMEM((half, wide), F32),
            pltpu.VMEM((2, n_test, half, wide), F32),
            pltpu.VMEM((n_dp, half, wide), F32),
            pltpu.VMEM((n_dp, n_test, half + 8, wide), F32),
            pltpu.VMEM((test_local, width, wide), F32),
            pltpu.VMEM((width, wide), F32),
            pltpu.VMEM((width, wide), F32),
            dma((n_loads,)),
            dma((2,)),
            dma((2, n_test)), dma((2, n_test)),
            dma, dma,
            dma((n_test - 1,)), dma((n_test - 1,)),
            dma((n_dp - 1,)), dma((n_dp - 1,)),
            dma((n_test, n_dp - 1)), dma((n_test, n_dp - 1)),
            dma, dma,
        ],
        compiler_params=pltpu.CompilerParams(
            collective_id=0, has_side_effects=True, vmem_limit_bytes=55200 * 1024
        ),
    )(lengths.reshape(1, 1), test_grads, train_inputs, train_grads, proj_in, proj_out)


def solution(mesh):
    return jax.shard_map(
        functools.partial(per_device, mesh.shape["dp"], mesh.shape["test"]),
        mesh=mesh,
        in_specs=(
            P(("grp", "dp", "test"), "seq", None),
            P(("grp", "dp", "test"), "seq", None),
            P(("grp", "dp", "test")),
            P(),
            P(),
            P(("grp", "dp", "test"), None),
        ),
        out_specs=P(("grp", "dp", "test"), None),
        check_vma=False,
    )
```
